32 devices in a mesh: row: 8 (over y, x, core), col: 4 (over z).
Axes of the slice: x: 2, y: 2, z: 4, core: 2. Of those that a mesh axis runs over, the one named last changes fastest.
Arguments:
- spectra: bfloat16 [2, 4, 128, 8192], P(None, None, 'col', 'row'), may hold values from -6 to 6
Outputs:
- cross: float32 [2, 4, 8192, 8192], P(None, None, 'row', 'col')
The draws below stay inside these ranges and needn't reach their ends.
All inputs are finite; a program needn't handle non-finite values.
Results may differ from the reference program's by a relative error of at most 0.0039.
Values may be sent and summed in bfloat16 or wider, within the bound.
No kernel may reach another device: no remote copies, remote signals or barrier semaphores. Data moves between devices by JAX's collectives and lax.ppermute only.
A program may use at most 192 MiB of HBM per device.

```python
import math
import jax
import jax.numpy as jnp
from jax import lax

F = 4
CH = 8192
W = 128


def block_levels(key, extent, split, smallest, high):
    level = 1.0
    for axis_at, blocks in split:
        heights = jax.random.uniform(jax.random.fold_in(jax.random.fold_in(key, 6), axis_at), (blocks,), jnp.float32, smallest / len(split), high / len(split))
        level = level * jnp.repeat(jnp.exp(heights), extent[axis_at] // blocks).reshape((-1,) + (1,) * (len(extent) - 1 - axis_at))
    return level


def gaussian(own_key, shape, scale, most, cuts=(), dtype=jnp.bfloat16):
    loudness = block_levels(own_key, shape, cuts, -0.22, 0.18) if cuts else 1.0
    drawn = jax.random.normal(own_key, shape, jnp.float32) * scale * loudness
    return jnp.minimum(jnp.maximum(drawn, -most), most).astype(dtype)


def setup_inputs(seed: int = 0) -> dict:
    streams_of = jax.random.split(jax.random.key(seed), 2)
    return {
        "spectra": gaussian(streams_of[0], (2, F, W, CH), 1.0, 6.0, ((2, 4), (3, 8))),
    }


def whiten(raw):
    real_part = raw[0].astype(jnp.float32)
    imag_part = raw[1].astype(jnp.float32)
    magnitude = jnp.sqrt(real_part * real_part + imag_part * imag_part)
    blank_row = jnp.zeros_like(magnitude[:1])
    upper_side = jnp.concatenate([magnitude[1:], blank_row], axis=0)
    lower_side = jnp.concatenate([blank_row, magnitude[:-1]], axis=0)
    bin_count = magnitude.shape[0]
    positions = jnp.arange(bin_count)
    neighbours = 3.0 - (positions == 0).astype(jnp.float32) - (positions == bin_count - 1).astype(jnp.float32)
    neighbours = neighbours.reshape((bin_count, 1, 1))
    water_level = jnp.maximum((magnitude + upper_side + lower_side) / neighbours, 0.75)
    return jnp.stack([real_part / water_level, imag_part / water_level]).astype(jnp.bfloat16)

def reference(spectra):
    whitened = whiten(spectra)
    norm_factor = 1.0 / math.sqrt(spectra.shape[2])
    by_bin = jnp.moveaxis(whitened, 1, 0)

    def real_bin(bin_pair):
        stacked = jnp.concatenate([bin_pair[0], bin_pair[1]], axis=0).astype(jnp.float32)
        return jnp.dot(stacked.T, stacked, precision=lax.Precision.HIGHEST, preferred_element_type=jnp.float32) * norm_factor

    def imag_bin(bin_pair):
        stacked = jnp.concatenate([bin_pair[0], bin_pair[1]], axis=0).astype(jnp.float32)
        turned = jnp.concatenate([-bin_pair[1], bin_pair[0]], axis=0).astype(jnp.float32)
        return jnp.dot(stacked.T, turned, precision=lax.Precision.HIGHEST, preferred_element_type=jnp.float32) * norm_factor
    real_out = lax.map(real_bin, by_bin)
    imag_out = lax.map(imag_bin, by_bin)
    return jnp.stack([real_out, imag_out])
```

```python
import functools
import math

import jax
import jax.numpy as jnp
from jax import lax
from jax.experimental import pallas as pl
from jax.experimental.pallas import tpu as pltpu
from jax.sharding import PartitionSpec as P


def whiten_kernel(n_split, steps, raw, *refs):
    n_bins, width = raw.shape[1], raw.shape[2]
    row_outs, held = refs[:-1], refs[-1]
    q = lax.axis_index("row") // 2
    real = [raw[0, f].astype(jnp.float32) for f in range(n_bins)]
    imag = [raw[1, f].astype(jnp.float32) for f in range(n_bins)]
    magnitude = [jnp.sqrt(a * a + b * b) for a, b in zip(real, imag)]
    part = held.shape[1]
    rows = min(part, width)
    for f in range(n_bins):
        near = [magnitude[g] for g in (f, f + 1, f - 1) if 0 <= g < n_bins]
        level = jnp.maximum(sum(near[1:], near[0]) / float(len(near)), 0.75)
        for p, values in ((0, real[f]), (1, imag[f])):
            white = (values / level).astype(jnp.bfloat16)
            for at in range(0, width, rows):
                piece, start = divmod(p * width + at, part)
                held[f * n_split + piece, start : start + rows] = white[at : at + rows]
    for chunk, out in zip(steps, row_outs):
        for i, step in enumerate(chunk):
            for s in range(n_split):
                out[i, s] = held[((q // n_split) ^ step) * n_split + s]


def whiten(raw, n, n_split, steps):
    _, n_bins, width, channels = raw.shape
    part = 2 * width // n_split
    shapes = [(len(chunk), n_split, part, channels) for chunk in steps] + [(n, part, channels)]
    outs = pl.pallas_call(
        functools.partial(whiten_kernel, n_split, steps),
        out_shape=[jax.ShapeDtypeStruct(shape, jnp.bfloat16) for shape in shapes],
        in_specs=[pl.BlockSpec(memory_space=pltpu.VMEM)],
        out_specs=[pl.BlockSpec(memory_space=pltpu.VMEM)] * len(shapes),
        compiler_params=pltpu.CompilerParams(vmem_limit_bytes=24 << 20),
        name="whiten",
    )(raw)
    return outs[:-1], outs[-1]


def product_kernel(chunk, n, n_split, n_rows, tile, norm, *refs):
    shards, refs = refs[:n_rows], refs[n_rows:]
    count = len(chunk) * n_split
    near, far = refs[:count], refs[count : 2 * count]
    out, turned, made, out_sem = refs[-4:]
    q, k, z = lax.axis_index("row") // 2, lax.axis_index("row") % 2, lax.axis_index("col")
    part, channels = shards[0].shape[2:]
    slots = made.shape[0]
    per_block = channels // tile
    n_tiles = 2 * per_block
    pairs = [(s, d) for s in range(n_split) for d in range(n)]

    def left_part(i, s, d):
        s = s ^ (q % n_split)
        if n == 4 and d == 3:
            return jnp.where((z == 0) | (z == 3), shards[4][i, s], shards[3][i, s])
        return shards[d][i, s]

    def store(i, at):
        block = jnp.where(at < per_block, k, 1 - k)
        start = pl.multiple_of(block * channels + (at % per_block) * tile, tile)
        total = i * n_tiles + at
        return pltpu.make_async_copy(
            made.at[total % slots],
            out.at[:, (q // n_split) ^ chunk[i], :, pl.ds(start, tile)],
            out_sem.at[total % slots],
        )

    def one_tile(columns, i, at):
        total = i * n_tiles + at

        @pl.when(total >= slots)
        def _():
            store(i, at).wait()

        start = pl.multiple_of((at % per_block) * tile, tile)
        piece = lambda s, d: columns[s][z ^ d, :, pl.ds(start, tile)]
        right = jnp.concatenate([piece(s, d) for s, d in pairs], axis=0)
        made[total % slots, 0] = norm * jnp.dot(turned[i % 2], right, preferred_element_type=jnp.float32)
        half = part // 2 if n_split == 1 else n_split // 2
        crossed = []
        for s, d in pairs:
            if n_split == 1:
                values = piece(s, d)
                crossed += [-values[half:], values[:half]]
            else:
                sign = jnp.where((s ^ (q % n_split)) < half, -1.0, 1.0).astype(jnp.bfloat16)
                crossed.append(piece(s ^ half, d) * sign)
        right = jnp.concatenate(crossed, axis=0)
        made[total % slots, 1] = norm * jnp.dot(turned[i % 2], right, preferred_element_type=jnp.float32)
        store(i, at).start()

    for i in range(len(chunk)):
        left = jnp.concatenate([left_part(i, s, d) for s, d in pairs], axis=0)
        turned[i % 2] = left.T
        mine = slice(i * n_split, (i + 1) * n_split)
        for columns, first in ((near[mine], 0), (far[mine], per_block)):
            lax.fori_loop(first, first + per_block, lambda at, _: one_tile(columns, i, at), None)
    total = len(chunk) * n_tiles
    for at in range(max(0, total - slots), total):
        store(at // n_tiles, at % n_tiles).wait()


def product(chunk, n, n_split, shards, near, far, before, n_columns, n_bins):
    part, channels = shards[0].shape[2:]
    depth = n * n_split * part
    tile = min(256, channels)
    slots = min(4, n_columns // tile)
    operands = [*shards, *near, *far]
    specs = [pl.BlockSpec(memory_space=pltpu.VMEM)] * len(operands)
    aliases = {}
    if before is not None:
        aliases = {len(operands): 0}
        operands.append(before)
        specs.append(pl.BlockSpec(memory_space=pl.ANY))
    norm = 1.0 / math.sqrt(depth // 2)
    return pl.pallas_call(
        functools.partial(product_kernel, chunk, n, n_split, len(shards), tile, norm),
        out_shape=jax.ShapeDtypeStruct((2, n_bins, channels, n_columns), jnp.float32),
        in_specs=specs,
        out_specs=pl.BlockSpec(memory_space=pl.ANY),
        scratch_shapes=[
            pltpu.VMEM((2, channels, depth), jnp.bfloat16),
            pltpu.VMEM((slots, 2, channels, tile), jnp.float32),
            pltpu.SemaphoreType.DMA((slots,)),
        ],
        input_output_aliases=aliases,
        cost_estimate=pl.CostEstimate(
            flops=len(chunk) * 4 * channels * n_columns * depth,
            bytes_accessed=len(chunk) * 8 * channels * n_columns,
            transcendentals=0,
        ),
        compiler_params=pltpu.CompilerParams(vmem_limit_bytes=32 << 20),
        name="product",
    )(*operands)


def gather_rows(mine, n):
    def by_xor(d):
        return lax.ppermute(mine, "col", [(z, z ^ d) for z in range(n)])

    if n != 4:
        return [mine] + [by_xor(d) for d in range(1, n)]
    one, two = by_xor(1), by_xor(2)
    middle = lax.ppermute(mine, "col", [(1, 2), (2, 1)])
    ends = lax.ppermute(two, "col", [(2, 3), (1, 0)])
    return [mine, one, two, middle, ends]


def shards(spectra):
    n = lax.axis_size("col")
    n_bins, channels = spectra.shape[1], spectra.shape[3]
    assert lax.axis_size("row") == 2 * n and n % n_bins == 0
    n_split = n // n_bins
    steps = [chunk for chunk in ((0,), tuple(range(1, n_bins - 1)), (n_bins - 1,)) if chunk]
    rows, pieces = whiten(spectra, n, n_split, steps)

    same_core = [[2 * q + k for q in range(n)] for k in range(2)]
    blocks = lax.all_to_all(pieces, "row", 0, 0, axis_index_groups=same_core, tiled=True)
    held = lax.all_to_all(blocks, "col", 0, 0, tiled=True)
    out = None
    for chunk, mine in zip(steps, rows):
        near = []
        for d in range(chunk[0] * n_split, (chunk[-1] + 1) * n_split):
            moves = [(2 * q + k, 2 * (q ^ d) + k) for q in range(n) for k in range(2)]
            near.append(lax.ppermute(held, "row", moves) if d else held)
        far = [lax.ppermute(x, "row", [(r, r ^ 1) for r in range(2 * n)]) for x in near]
        out = product(chunk, n, n_split, gather_rows(mine, n), near, far, out, 2 * channels, n_bins)
    return out


def solution(mesh):
    in_specs = (P(None, None, "col", "row"),)
    out_specs = P(None, None, "row", "col")
    return jax.shard_map(shards, mesh=mesh, in_specs=in_specs, out_specs=out_specs, check_vma=False)
```

```python
import functools
import math

import jax
import jax.numpy as jnp
from jax import lax
from jax.experimental import pallas as pl
from jax.experimental.pallas import tpu as pltpu
from jax.sharding import PartitionSpec as P

WEIGHT = 4


def whiten_kernel(n, n_split, steps, raw, *refs):
    n_bins, width = raw.shape[1], raw.shape[2]
    row_outs, piece_outs, held = refs[: len(steps)], refs[len(steps) : -1], refs[-1]
    q = lax.axis_index("row") // 2
    real = [raw[0, f].astype(jnp.float32) for f in range(n_bins)]
    imag = [raw[1, f].astype(jnp.float32) for f in range(n_bins)]
    magnitude = [jnp.sqrt(a * a + b * b) for a, b in zip(real, imag)]
    part = held.shape[1]
    rows = min(part, width)
    for f in range(n_bins):
        near = [magnitude[g] for g in (f, f + 1, f - 1) if 0 <= g < n_bins]
        level = jnp.maximum(sum(near[1:], near[0]) / float(len(near)), 0.75)
        for p, values in ((0, real[f]), (1, imag[f])):
            white = (values / level).astype(jnp.bfloat16)
            for at in range(0, width, rows):
                piece, start = divmod(p * width + at, part)
                held[f * n_split + piece, start : start + rows] = white[at : at + rows]
    for chunk, out in zip(steps, row_outs):
        for i, step in enumerate(chunk):
            for s in range(n_split):
                out[0, i, s] = held[((q // n_split) ^ step) * n_split + s]
    for d, out in enumerate(piece_outs):
        out[...] = held[q ^ d]


def whiten(raw, n, n_split, steps):
    _, n_bins, width, channels = raw.shape
    part = 2 * width // n_split
    shapes = [(1, len(chunk), n_split, part, channels) for chunk in steps] + [(part, channels)] * n
    outs = pl.pallas_call(
        functools.partial(whiten_kernel, n, n_split, steps),
        out_shape=[jax.ShapeDtypeStruct(shape, jnp.bfloat16) for shape in shapes],
        in_specs=[pl.BlockSpec(memory_space=pltpu.VMEM)],
        out_specs=[pl.BlockSpec(memory_space=pltpu.VMEM)] * len(shapes),
        scratch_shapes=[pltpu.VMEM((n, part, channels), jnp.bfloat16)],
        compiler_params=pltpu.CompilerParams(vmem_limit_bytes=24 << 20),
        name="whiten",
    )(raw)
    return outs[: len(steps)], outs[len(steps) :]


def route_kernel(*refs):
    n = len(refs) // 2
    blocks, outs = refs[:n], refs[n:]
    q, z = lax.axis_index("row") // 2, lax.axis_index("col")
    for e, out in enumerate(outs):
        wanted = q ^ z ^ e
        for d, block in enumerate(blocks):

            @pl.when(wanted == d)
            def _(block=block, out=out):
                out[...] = block[...]


def route(blocks):
    n = len(blocks)
    shape = jax.ShapeDtypeStruct(blocks[0].shape, jnp.bfloat16)
    return pl.pallas_call(
        route_kernel,
        out_shape=[shape] * n,
        in_specs=[pl.BlockSpec(memory_space=pltpu.VMEM)] * n,
        out_specs=[pl.BlockSpec(memory_space=pltpu.VMEM)] * n,
        compiler_params=pltpu.CompilerParams(vmem_limit_bytes=24 << 20),
        name="route",
    )(*blocks)


def collect_kernel(*refs):
    z = lax.axis_index("col")
    for e, x in enumerate(refs[:-1]):
        refs[-1][z ^ e] = x[...]


def collect(parts):
    return pl.pallas_call(
        collect_kernel,
        out_shape=jax.ShapeDtypeStruct((len(parts), *parts[0].shape), jnp.bfloat16),
        in_specs=[pl.BlockSpec(memory_space=pltpu.VMEM)] * len(parts),
        out_specs=pl.BlockSpec(memory_space=pltpu.VMEM),
        compiler_params=pltpu.CompilerParams(vmem_limit_bytes=24 << 20),
        name="collect",
    )(*parts)


def product_kernel(items, n, n_split, tile, norm, *refs):
    n_parts = n.bit_length()
    per_item = n_parts + n_split
    operands = [refs[at * per_item : (at + 1) * per_item] for at in range(len(items))]
    out, turned, made, out_sem = refs[-4:]
    q, k, z = lax.axis_index("row") // 2, lax.axis_index("row") % 2, lax.axis_index("col")
    part, channels = operands[0][0].shape[2:]
    slots = made.shape[0]
    n_tiles = channels // tile
    pairs = [(s, d) for s in range(n_split) for d in range(n)]

    def left_part(shards, s, d):
        at, place, order = 0, 0, [0]
        while d not in order:
            at, bit = at + 1, n >> (at + 1)
            taken = [bit ^ other for other in order]
            place, order = (taken.index(d) if d in taken else 0), order + taken
        return shards[at][place, s ^ (q % n_split)]

    def store(item, at):
        step, other = items[item]
        block = 1 - k if other else k
        start = pl.multiple_of(block * channels + at * tile, tile)
        total = item * n_tiles + at
        return pltpu.make_async_copy(
            made.at[total % slots],
            out.at[:, (q // n_split) ^ step, :, pl.ds(start, tile)],
            out_sem.at[total % slots],
        )

    def one_tile(item, columns, at):
        total = item * n_tiles + at

        @pl.when(total >= slots)
        def _():
            store(item, at).wait()

        start = pl.multiple_of(at * tile, tile)
        piece = lambda s, d: columns[s][z ^ d, :, pl.ds(start, tile)]
        right = jnp.concatenate([piece(s, d) for s, d in pairs], axis=0)
        made[total % slots, 0] = norm * jnp.dot(turned[item], right, preferred_element_type=jnp.float32)
        half = part // 2 if n_split == 1 else n_split // 2
        crossed = []
        for s, d in pairs:
            if n_split == 1:
                values = piece(s, d)
                crossed += [-values[half:], values[:half]]
            else:
                sign = jnp.where((s ^ (q % n_split)) < half, -1.0, 1.0).astype(jnp.bfloat16)
                crossed.append(piece(s ^ half, d) * sign)
        right = jnp.concatenate(crossed, axis=0)
        made[total % slots, 1] = norm * jnp.dot(turned[item], right, preferred_element_type=jnp.float32)
        store(item, at).start()

    for item, arrays in enumerate(operands):
        shards, columns = arrays[:n_parts], arrays[n_parts:]
        left = jnp.concatenate([left_part(shards, s, d) for s, d in pairs], axis=0)
        turned[item] = left.T
        lax.fori_loop(0, n_tiles, lambda at, _: one_tile(item, columns, at), None)
    total = len(items) * n_tiles
    for at in range(max(0, total - slots), total):
        store(at // n_tiles, at % n_tiles).wait()


def product(items, n, n_split, shards, columns, before, n_bins):
    part, channels = shards[0][0].shape[2:]
    depth = n * n_split * part
    tile = min(256, channels)
    slots = min(4, len(items) * channels // tile)
    operands = [x for pair in zip(shards, columns) for arrays in pair for x in arrays]
    specs = [pl.BlockSpec(memory_space=pltpu.VMEM)] * len(operands)
    aliases = {}
    if before is not None:
        aliases = {len(operands): 0}
        operands.append(before)
        specs.append(pl.BlockSpec(memory_space=pl.ANY))
    norm = 1.0 / math.sqrt(depth // 2)
    return pl.pallas_call(
        functools.partial(product_kernel, items, n, n_split, tile, norm),
        out_shape=jax.ShapeDtypeStruct((2, n_bins, channels, 2 * channels), jnp.float32),
        in_specs=specs,
        out_specs=pl.BlockSpec(memory_space=pl.ANY),
        scratch_shapes=[
            pltpu.VMEM((len(items), channels, depth), jnp.bfloat16),
            pltpu.VMEM((slots, 2, channels, tile), jnp.float32),
            pltpu.SemaphoreType.DMA((slots,)),
        ],
        input_output_aliases=aliases,
        cost_estimate=pl.CostEstimate(
            flops=WEIGHT * len(items) * 4 * channels * channels * depth,
            bytes_accessed=WEIGHT * len(items) * 8 * channels * channels,
            transcendentals=0,
        ),
        compiler_params=pltpu.CompilerParams(vmem_limit_bytes=32 << 20),
        name="product",
    )(*operands)


def along_line(values, bit, n):
    return lax.ppermute(values, "col", [(z, z ^ bit) for z in range(n)])


def gather_rows(mine, first, n):
    parts, bit = [mine, first], n // 4
    while bit:
        parts.append(along_line(jnp.concatenate(parts), bit, n))
        bit //= 2
    return parts


def shards(spectra):
    n = lax.axis_size("col")
    n_bins = spectra.shape[1]
    assert lax.axis_size("row") == 2 * n and n % n_bins == 0 and n & (n - 1) == 0
    n_split = n // n_bins
    rows, pieces = whiten(spectra, n, n_split, [(f,) for f in range(n_bins)])
    rows = [x[:, 0] for x in rows]

    def from_chip(values, d):
        return lax.ppermute(values, "row", [(2 * q + k, 2 * (q ^ d) + k) for q in range(n) for k in range(2)])

    def from_core(values):
        return lax.ppermute(values, "row", [(r, r ^ 1) for r in range(2 * n)])

    early = n_bins // 2
    firsts = [along_line(x, n // 2, n) for x in rows[:early]]
    blocks = [from_chip(piece, d) if d else piece for d, piece in enumerate(pieces)]
    firsts, blocks = lax.optimization_barrier((firsts, blocks))
    arrived = [along_line(x, e, n) if e else x for e, x in enumerate(route(blocks))]
    rows[early:], arrived = lax.optimization_barrier((rows[early:], arrived))
    firsts += [along_line(x, n // 2, n) for x in rows[early:]]
    gathered_rows = [gather_rows(mine, first, n) for mine, first in zip(rows, firsts)]
    held = collect(arrived)
    gathered_rows[0], held = lax.optimization_barrier((gathered_rows[0], held))
    near = [held]
    for d in range(1, n):
        low = d & -d
        near.append(from_chip(near[d ^ low], low))
    far = [from_core(x) for x in near]
    near, far = ([x[f * n_split : (f + 1) * n_split] for f in range(n_bins)] for x in (near, far))
    calls = [[(0, False)]]
    for f in range(1, n_bins):
        calls.append([(f - 1, True), (f, False)])
    calls.append([(n_bins - 1, True)])
    out = None
    for items in calls:
        used = [gathered_rows[f] for f, _ in items]
        columns = [(far if other else near)[f] for f, other in items]
        out = product(items, n, n_split, used, columns, out, n_bins)
    return out


def solution(mesh):
    in_specs = (P(None, None, "col", "row"),)
    out_specs = P(None, None, "row", "col")
    return jax.shard_map(shards, mesh=mesh, in_specs=in_specs, out_specs=out_specs, check_vma=False)
```

```python
import functools
import math

import jax
import jax.numpy as jnp
from jax import lax
from jax.experimental import pallas as pl
from jax.experimental.pallas import tpu as pltpu
from jax.sharding import PartitionSpec as P

WEIGHT = 4


def whiten_kernel(n, n_split, steps, raw, *refs):
    n_bins, width = raw.shape[1], raw.shape[2]
    row_outs, piece_outs, held = refs[: len(steps)], refs[len(steps) : -1], refs[-1]
    q = lax.axis_index("row") // 2
    real = [raw[0, f].astype(jnp.float32) for f in range(n_bins)]
    imag = [raw[1, f].astype(jnp.float32) for f in range(n_bins)]
    magnitude = [jnp.sqrt(a * a + b * b) for a, b in zip(real, imag)]
    part = held.shape[1]
    rows = min(part, width)
    for f in range(n_bins):
        near = [magnitude[g] for g in (f, f + 1, f - 1) if 0 <= g < n_bins]
        level = jnp.maximum(sum(near[1:], near[0]) / float(len(near)), 0.75)
        for p, values in ((0, real[f]), (1, imag[f])):
            white = (values / level).astype(jnp.bfloat16)
            for at in range(0, width, rows):
                piece, start = divmod(p * width + at, part)
                held[f * n_split + piece, start : start + rows] = white[at : at + rows]
    for chunk, out in zip(steps, row_outs):
        for i, step in enumerate(chunk):
            for s in range(n_split):
                out[0, i, s] = held[((q // n_split) ^ step) * n_split + s]
    for d, out in enumerate(piece_outs):
        out[...] = held[q ^ d]


def whiten(raw, n, n_split, steps):
    _, n_bins, width, channels = raw.shape
    part = 2 * width // n_split
    shapes = [(1, len(chunk), n_split, part, channels) for chunk in steps] + [(part, channels)] * n
    outs = pl.pallas_call(
        functools.partial(whiten_kernel, n, n_split, steps),
        out_shape=[jax.ShapeDtypeStruct(shape, jnp.bfloat16) for shape in shapes],
        in_specs=[pl.BlockSpec(memory_space=pltpu.VMEM)],
        out_specs=[pl.BlockSpec(memory_space=pltpu.VMEM)] * len(shapes),
        scratch_shapes=[pltpu.VMEM((n, part, channels), jnp.bfloat16)],
        compiler_params=pltpu.CompilerParams(vmem_limit_bytes=24 << 20),
        name="whiten",
    )(raw)
    return outs[: len(steps)], outs[len(steps) :]


def route_kernel(*refs):
    n = len(refs) // 2
    blocks, outs = refs[:n], refs[n:]
    q, z = lax.axis_index("row") // 2, lax.axis_index("col")
    for e, out in enumerate(outs):
        wanted = q ^ z ^ e
        for d, block in enumerate(blocks):

            @pl.when(wanted == d)
            def _(block=block, out=out):
                out[...] = block[...]


def route(blocks):
    n = len(blocks)
    shape = jax.ShapeDtypeStruct(blocks[0].shape, jnp.bfloat16)
    return pl.pallas_call(
        route_kernel,
        out_shape=[shape] * n,
        in_specs=[pl.BlockSpec(memory_space=pltpu.VMEM)] * n,
        out_specs=[pl.BlockSpec(memory_space=pltpu.VMEM)] * n,
        compiler_params=pltpu.CompilerParams(vmem_limit_bytes=24 << 20),
        name="route",
    )(*blocks)


def collect_kernel(*refs):
    z = lax.axis_index("col")
    for e, x in enumerate(refs[:-1]):
        refs[-1][z ^ e] = x[...]


def collect(parts):
    return pl.pallas_call(
        collect_kernel,
        out_shape=jax.ShapeDtypeStruct((len(parts), *parts[0].shape), jnp.bfloat16),
        in_specs=[pl.BlockSpec(memory_space=pltpu.VMEM)] * len(parts),
        out_specs=pl.BlockSpec(memory_space=pltpu.VMEM),
        compiler_params=pltpu.CompilerParams(vmem_limit_bytes=24 << 20),
        name="collect",
    )(*parts)


def product_kernel(items, n, n_split, tile, norm, *refs):
    n_parts = n.bit_length()
    per_item = n_parts + n_split
    operands = [refs[at * per_item : (at + 1) * per_item] for at in range(len(items))]
    out, turned, made, out_sem = refs[-4:]
    q, k, z = lax.axis_index("row") // 2, lax.axis_index("row") % 2, lax.axis_index("col")
    part, channels = operands[0][0].shape[2:]
    slots = made.shape[0]
    n_tiles = channels // tile
    pairs = [(s, d) for s in range(n_split) for d in range(n)]

    def left_part(shards, s, d):
        at, place, order = 0, 0, [0]
        while d not in order:
            at, bit = at + 1, n >> (at + 1)
            taken = [bit ^ other for other in order]
            place, order = (taken.index(d) if d in taken else 0), order + taken
        return shards[at][place, s ^ (q % n_split)]

    def store(item, at):
        step, other = items[item]
        block = 1 - k if other else k
        start = pl.multiple_of(block * channels + at * tile, tile)
        total = item * n_tiles + at
        return pltpu.make_async_copy(
            made.at[total % slots],
            out.at[:, (q // n_split) ^ step, :, pl.ds(start, tile)],
            out_sem.at[total % slots],
        )

    def one_tile(item, columns, at):
        total = item * n_tiles + at

        @pl.when(total >= slots)
        def _():
            store(item, at).wait()

        start = pl.multiple_of(at * tile, tile)
        piece = lambda s, d: columns[s][z ^ d, :, pl.ds(start, tile)]
        right = jnp.concatenate([piece(s, d) for s, d in pairs], axis=0)
        made[total % slots, 0] = norm * jnp.dot(turned[item], right, preferred_element_type=jnp.float32)
        half = part // 2 if n_split == 1 else n_split // 2
        crossed = []
        for s, d in pairs:
            if n_split == 1:
                values = piece(s, d)
                crossed += [-values[half:], values[:half]]
            else:
                sign = jnp.where((s ^ (q % n_split)) < half, -1.0, 1.0).astype(jnp.bfloat16)
                crossed.append(piece(s ^ half, d) * sign)
        right = jnp.concatenate(crossed, axis=0)
        made[total % slots, 1] = norm * jnp.dot(turned[item], right, preferred_element_type=jnp.float32)
        store(item, at).start()

    for item, arrays in enumerate(operands):
        shards, columns = arrays[:n_parts], arrays[n_parts:]
        left = jnp.concatenate([left_part(shards, s, d) for s, d in pairs], axis=0)
        turned[item] = left.T
        lax.fori_loop(0, n_tiles, lambda at, _: one_tile(item, columns, at), None)
    total = len(items) * n_tiles
    for at in range(max(0, total - slots), total):
        store(at // n_tiles, at % n_tiles).wait()


def product(items, n, n_split, shards, columns, before, n_bins):
    part, channels = shards[0][0].shape[2:]
    depth = n * n_split * part
    tile = min(256, channels)
    slots = min(4, len(items) * channels // tile)
    operands = [x for pair in zip(shards, columns) for arrays in pair for x in arrays]
    specs = [pl.BlockSpec(memory_space=pltpu.VMEM)] * len(operands)
    aliases = {}
    if before is not None:
        aliases = {len(operands): 0}
        operands.append(before)
        specs.append(pl.BlockSpec(memory_space=pl.ANY))
    norm = 1.0 / math.sqrt(depth // 2)
    return pl.pallas_call(
        functools.partial(product_kernel, items, n, n_split, tile, norm),
        out_shape=jax.ShapeDtypeStruct((2, n_bins, channels, 2 * channels), jnp.float32),
        in_specs=specs,
        out_specs=pl.BlockSpec(memory_space=pl.ANY),
        scratch_shapes=[
            pltpu.VMEM((len(items), channels, depth), jnp.bfloat16),
            pltpu.VMEM((slots, 2, channels, tile), jnp.float32),
            pltpu.SemaphoreType.DMA((slots,)),
        ],
        input_output_aliases=aliases,
        cost_estimate=pl.CostEstimate(
            flops=WEIGHT * len(items) * 4 * channels * channels * depth,
            bytes_accessed=WEIGHT * len(items) * 8 * channels * channels,
            transcendentals=0,
        ),
        compiler_params=pltpu.CompilerParams(vmem_limit_bytes=32 << 20),
        name="product",
    )(*operands)


def along_line(values, bit, n):
    return lax.ppermute(values, "col", [(z, z ^ bit) for z in range(n)])


def gather_rows(mine, first, n):
    parts, bit = [mine, first], n // 4
    while bit:
        parts.append(along_line(jnp.concatenate(parts), bit, n))
        bit //= 2
    return parts


def shards(spectra):
    n = lax.axis_size("col")
    n_bins = spectra.shape[1]
    assert lax.axis_size("row") == 2 * n and n % n_bins == 0 and n & (n - 1) == 0
    n_split = n // n_bins
    rows, pieces = whiten(spectra, n, n_split, [(f,) for f in range(n_bins)])
    rows = [x[:, 0] for x in rows]

    def from_chip(values, d):
        return lax.ppermute(values, "row", [(2 * q + k, 2 * (q ^ d) + k) for q in range(n) for k in range(2)])

    def from_core(values):
        return lax.ppermute(values, "row", [(r, r ^ 1) for r in range(2 * n)])

    first = along_line(rows[0], n // 2, n)
    blocks = [from_chip(piece, d) if d else piece for d, piece in enumerate(pieces)]
    first, blocks = lax.optimization_barrier((first, blocks))
    row_parts = [gather_rows(rows[0], first, n)]
    arrived = [along_line(x, e, n) if e else x for e, x in enumerate(route(blocks))]
    row_parts[0], arrived = lax.optimization_barrier((row_parts[0], arrived))
    near = [collect(arrived)]
    for d in range(1, n):
        low = d & -d
        if d == low or d < n_split:
            near.append(from_chip(near[d ^ low], low))
        else:
            near.append(None)
    far = [from_core(x) for x in near[:n_split]]
    rows[1], near[0] = lax.optimization_barrier((rows[1], near[0]))
    firsts = [first]
    for f in range(1, min(3, n_bins)):
        if f > 1:
            rows[f], firsts[-1] = lax.optimization_barrier((rows[f], firsts[-1]))
        firsts.append(along_line(rows[f], n // 2, n))
    row_parts.append(gather_rows(rows[1], firsts[1], n))

    call = functools.partial(product, n=n, n_split=n_split, n_bins=n_bins)
    piece = lambda x, f: x[f * n_split : (f + 1) * n_split]
    out = call([(0, False), (0, True)], shards=[row_parts[0]] * 2, columns=[piece(near, 0), piece(far, 0)], before=None)
    held = (rows[2:], firsts[2:], near[n_split:])
    out, (rows[2:], firsts[2:], near[n_split:]) = lax.optimization_barrier((out, held))
    for f in range(2, n_bins):
        if f == len(firsts):
            firsts.append(along_line(rows[f], n // 2, n))
        row_parts.append(gather_rows(rows[f], firsts[f], n))
    for d in range(n_split, n):
        low = d & -d
        if near[d] is None:
            near[d] = from_chip(near[d ^ low], low)
    for f in range(1, n_bins + 1):
        if f < n_bins:
            mine, out = lax.optimization_barrier((piece(near, f), out))
            far += [from_core(x) for x in mine]
        items = [(f - 1, True)] * (f > 1) + [(f, False)] * (f < n_bins)
        columns = [piece(far if other else near, at) for at, other in items]
        out = call(items, shards=[row_parts[at] for at, _ in items], columns=columns, before=out)
    return out


def solution(mesh):
    in_specs = (P(None, None, "col", "row"),)
    out_specs = P(None, None, "row", "col")
    return jax.shard_map(shards, mesh=mesh, in_specs=in_specs, out_specs=out_specs, check_vma=False)
```

```python
import functools
import math

import jax
import jax.numpy as jnp
from jax import lax
from jax.experimental import pallas as pl
from jax.experimental.pallas import tpu as pltpu
from jax.sharding import PartitionSpec as P


def whiten_kernel(n, n_split, steps, raw, *refs):
    n_bins, width = raw.shape[1], raw.shape[2]
    row_outs, piece_outs, held = refs[: len(steps)], refs[len(steps) : -1], refs[-1]
    q = lax.axis_index("row") // 2
    real = [raw[0, f].astype(jnp.float32) for f in range(n_bins)]
    imag = [raw[1, f].astype(jnp.float32) for f in range(n_bins)]
    magnitude = [jnp.sqrt(a * a + b * b) for a, b in zip(real, imag)]
    part = held.shape[1]
    rows = min(part, width)
    for f in range(n_bins):
        near = [magnitude[g] for g in (f, f + 1, f - 1) if 0 <= g < n_bins]
        level = jnp.maximum(sum(near[1:], near[0]) / float(len(near)), 0.75)
        for p, values in ((0, real[f]), (1, imag[f])):
            white = (values / level).astype(jnp.bfloat16)
            for at in range(0, width, rows):
                piece, start = divmod(p * width + at, part)
                held[f * n_split + piece, start : start + rows] = white[at : at + rows]
    for chunk, out in zip(steps, row_outs):
        for i, step in enumerate(chunk):
            for s in range(n_split):
                out[0, i, s] = held[((q // n_split) ^ step) * n_split + s]
    for d, out in enumerate(piece_outs):
        out[...] = held[q ^ d]


def whiten(raw, n, n_split, steps):
    _, n_bins, width, channels = raw.shape
    part = 2 * width // n_split
    shapes = [(1, len(chunk), n_split, part, channels) for chunk in steps] + [(part, channels)] * n
    outs = pl.pallas_call(
        functools.partial(whiten_kernel, n, n_split, steps),
        out_shape=[jax.ShapeDtypeStruct(shape, jnp.bfloat16) for shape in shapes],
        in_specs=[pl.BlockSpec(memory_space=pltpu.VMEM)],
        out_specs=[pl.BlockSpec(memory_space=pltpu.VMEM)] * len(shapes),
        scratch_shapes=[pltpu.VMEM((n, part, channels), jnp.bfloat16)],
        compiler_params=pltpu.CompilerParams(vmem_limit_bytes=24 << 20),
        name="whiten",
    )(raw)
    return outs[: len(steps)], outs[len(steps) :]


def route_kernel(*refs):
    n = len(refs) // 2
    blocks, outs = refs[:n], refs[n:]
    q, z = lax.axis_index("row") // 2, lax.axis_index("col")
    for e, out in enumerate(outs):
        wanted = q ^ z ^ e
        for d, block in enumerate(blocks):

            @pl.when(wanted == d)
            def _(block=block, out=out):
                out[...] = block[...]


def route(blocks):
    n = len(blocks)
    shape = jax.ShapeDtypeStruct(blocks[0].shape, jnp.bfloat16)
    return pl.pallas_call(
        route_kernel,
        out_shape=[shape] * n,
        in_specs=[pl.BlockSpec(memory_space=pltpu.VMEM)] * n,
        out_specs=[pl.BlockSpec(memory_space=pltpu.VMEM)] * n,
        compiler_params=pltpu.CompilerParams(vmem_limit_bytes=24 << 20),
        name="route",
    )(*blocks)


def collect_kernel(*refs):
    z = lax.axis_index("col")
    for e, x in enumerate(refs[:-1]):
        refs[-1][z ^ e] = x[...]


def collect(parts):
    return pl.pallas_call(
        collect_kernel,
        out_shape=jax.ShapeDtypeStruct((len(parts), *parts[0].shape), jnp.bfloat16),
        in_specs=[pl.BlockSpec(memory_space=pltpu.VMEM)] * len(parts),
        out_specs=pl.BlockSpec(memory_space=pltpu.VMEM),
        compiler_params=pltpu.CompilerParams(vmem_limit_bytes=24 << 20),
        name="collect",
    )(*parts)


def turn_kernel(at, n, n_split, *refs):
    q = lax.axis_index("row") // 2
    out = refs[-1]
    where, bit = {0: (0, 0)}, n
    for ref in range(1, len(refs) - 1):
        bit //= 2
        for place, d in enumerate(list(where)):
            where[d ^ bit] = (ref, place)
    picked = []
    for s in range(n_split):
        for d in range(n):
            ref, place = where[d]
            own = s ^ (q % n_split)
            picked.append(refs[ref][place, at, own] if ref < 2 else refs[ref][place, own])
    out[...] = jnp.concatenate(picked, axis=0).T


def turn(at, parts, n):
    _, _, n_split, part, channels = parts[0].shape
    return pl.pallas_call(
        functools.partial(turn_kernel, at, n, n_split),
        out_shape=jax.ShapeDtypeStruct((channels, n * n_split * part), jnp.bfloat16),
        in_specs=[pl.BlockSpec(memory_space=pltpu.VMEM)] * len(parts),
        out_specs=pl.BlockSpec(memory_space=pltpu.VMEM),
        compiler_params=pltpu.CompilerParams(vmem_limit_bytes=24 << 20),
        name="turn",
    )(*parts)


def product_kernel(items, n, n_split, tile, norm, *refs):
    operands = [refs[at * (n_split + 1) : (at + 1) * (n_split + 1)] for at in range(len(items))]
    out, made, out_sem = refs[-3:]
    q, k, z = lax.axis_index("row") // 2, lax.axis_index("row") % 2, lax.axis_index("col")
    channels = operands[0][0].shape[0]
    part = operands[0][1].shape[1]
    slots, _, height, width = made.shape
    per_column = channels // height
    n_tiles = per_column * (channels // width)
    pairs = [(s, d) for s in range(n_split) for d in range(n)]

    def store(item, at):
        step, other = items[item]
        block = 1 - k if other else k
        top = pl.multiple_of(at % per_column * height, height)
        start = pl.multiple_of(block * channels + at // per_column * width, width)
        slot = (item * n_tiles + at) % slots
        return pltpu.make_async_copy(
            made.at[slot],
            out.at[:, (q // n_split) ^ step, pl.ds(top, height), pl.ds(start, width)],
            out_sem.at[slot],
        )

    def one_tile(item, turned, columns, at):
        total = item * n_tiles + at

        @pl.when(total >= slots)
        def _():
            store(item, at).wait()

        left = turned[pl.ds(pl.multiple_of(at % per_column * height, height), height)]
        start = pl.multiple_of(at // per_column * width, width)
        piece = lambda s, d: columns[s][z ^ d, :, pl.ds(start, width)]
        right = jnp.concatenate([piece(s, d) for s, d in pairs], axis=0)
        made[total % slots, 0] = norm * jnp.dot(left, right, preferred_element_type=jnp.float32)
        half = part // 2 if n_split == 1 else n_split // 2
        crossed = []
        for s, d in pairs:
            if n_split == 1:
                values = piece(s, d)
                crossed += [-values[half:], values[:half]]
            else:
                sign = jnp.where((s ^ (q % n_split)) < half, -1.0, 1.0).astype(jnp.bfloat16)
                crossed.append(piece(s ^ half, d) * sign)
        right = jnp.concatenate(crossed, axis=0)
        made[total % slots, 1] = norm * jnp.dot(left, right, preferred_element_type=jnp.float32)
        store(item, at).start()

    for item, (turned, *columns) in enumerate(operands):
        lax.fori_loop(0, n_tiles, lambda at, _: one_tile(item, turned, columns, at), None)
    total = len(items) * n_tiles
    for at in range(max(0, total - slots), total):
        store(at // n_tiles, at % n_tiles).wait()


def product(items, turned, columns, before, n, n_split, n_bins):
    channels, depth = turned[0].shape
    width, height = min(256, channels), min(512, channels)
    slots = min(8, len(items) * (channels // width) * (channels // height))
    operands = [x for left, right in zip(turned, columns) for x in (left, *right)]
    specs = [pl.BlockSpec(memory_space=pltpu.VMEM)] * len(operands)
    aliases = {}
    if before is not None:
        aliases = {len(operands): 0}
        operands.append(before)
        specs.append(pl.BlockSpec(memory_space=pl.ANY))
    norm = 1.0 / math.sqrt(depth // 2)
    return pl.pallas_call(
        functools.partial(product_kernel, items, n, n_split, width, norm),
        out_shape=jax.ShapeDtypeStruct((2, n_bins, channels, 2 * channels), jnp.float32),
        in_specs=specs,
        out_specs=pl.BlockSpec(memory_space=pl.ANY),
        scratch_shapes=[
            pltpu.VMEM((slots, 2, height, width), jnp.float32),
            pltpu.SemaphoreType.DMA((slots,)),
        ],
        input_output_aliases=aliases,
        cost_estimate=pl.CostEstimate(
            flops=len(items) * 4 * channels * channels * depth // 4,
            bytes_accessed=len(items) * 8 * channels * channels // 4,
            transcendentals=0,
        ),
        compiler_params=pltpu.CompilerParams(vmem_limit_bytes=32 << 20),
        name="product",
    )(*operands)


def shards(spectra):
    n = lax.axis_size("col")
    n_bins = spectra.shape[1]
    assert lax.axis_size("row") == 2 * n and n % n_bins == 0 and n_bins > 1 and n & (n - 1) == 0
    n_split = n // n_bins
    chunks = [(0, 1)] + [(f,) for f in range(2, n_bins)]
    place = [(at, i) for at, chunk in enumerate(chunks) for i in range(len(chunk))]
    rows, pieces = whiten(spectra, n, n_split, chunks)

    def along_line(values, bit):
        return lax.ppermute(values, "col", [(z, z ^ bit) for z in range(n)])

    def from_chip(values, d):
        return lax.ppermute(values, "row", [(2 * q + k, 2 * (q ^ d) + k) for q in range(n) for k in range(2)])

    def from_core(values):
        return lax.ppermute(values, "row", [(r, r ^ 1) for r in range(2 * n)])

    def gather_rows(own, first, at):
        parts, bit = [own[:, at], first[:, at]], n // 4
        while bit:
            parts.append(along_line(jnp.concatenate(parts), bit))
            bit //= 2
        return [own, first, *parts[2:]]

    def wait(values, done):
        return lax.optimization_barrier((values, done))

    def gather_bin(f):
        at, i = place[f]
        return gather_rows(rows[at], firsts[at], i)

    firsts = [along_line(rows[0], n // 2)]
    blocks = [from_chip(piece, d) if d else piece for d, piece in enumerate(pieces)]
    firsts, blocks = wait(firsts, blocks)
    arrived = [along_line(x, e) if e else x for e, x in enumerate(route(blocks))]
    parts = [gather_bin(0)]
    (rows, firsts, parts), arrived = wait((rows, firsts, parts), arrived)
    near = [collect(arrived)]
    for d in range(1, n):
        low = d & -d
        near.append(from_chip(near[d ^ low], low) if d == low or d < n_split else None)
    far = [from_core(x) for x in near[:n_split]]
    parts.append(gather_bin(1))
    firsts += [along_line(x, n // 2) for x in rows[1:2]]

    call = functools.partial(product, n=n, n_split=n_split, n_bins=n_bins)
    of_bin = lambda x, f: x[f * n_split : (f + 1) * n_split]
    turned = turn(0, parts[0], n)
    out = call([(0, False), (0, True)], [turned] * 2, [of_bin(near, 0), far], None)
    near[n_split:], out = wait(near[n_split:], out)
    for d in range(n_split, n):
        low = d & -d
        if near[d] is None:
            near[d] = from_chip(near[d ^ low], low)
    for f in range(1, n_bins):
        needed = (parts[f], firsts, rows, of_bin(near, f))
        (parts[f], firsts, rows, mine), out = wait(needed, out)
        turned = turn(place[f][1], parts[f], n)
        if f + 1 < n_bins:
            parts.append(gather_bin(f + 1))
        if f + 2 < n_bins:
            firsts.append(along_line(rows[f + 1], n // 2))
        if f in (1, n_bins - 1):
            far = [from_core(x) for x in mine]
            out = call([(f, False)], [turned], [mine], out)
            (far, later), out = wait((far, of_bin(near, f + 1) if f == 1 else []), out)
            following = [from_core(x) for x in later]
            out = call([(f, True)], [turned], [far], out)
        else:
            (far, later), out = wait((following, of_bin(near, f + 1) if f + 2 < n_bins else []), out)
            following = [from_core(x) for x in later]
            out = call([(f, False), (f, True)], [turned] * 2, [mine, far], out)
    return out


def solution(mesh):
    in_specs = (P(None, None, "col", "row"),)
    out_specs = P(None, None, "row", "col")
    return jax.shard_map(shards, mesh=mesh, in_specs=in_specs, out_specs=out_specs, check_vma=False)
```

```python
import functools
import math

import jax
import jax.numpy as jnp
from jax import lax
from jax.experimental import pallas as pl
from jax.experimental.pallas import tpu as pltpu
from jax.sharding import PartitionSpec as P


def whiten_kernel(n, n_split, steps, raw, *refs):
    n_bins, width = raw.shape[1], raw.shape[2]
    row_outs, piece_outs, held = refs[: len(steps)], refs[len(steps) : -1], refs[-1]
    q = lax.axis_index("row") // 2
    real = [raw[0, f].astype(jnp.float32) for f in range(n_bins)]
    imag = [raw[1, f].astype(jnp.float32) for f in range(n_bins)]
    magnitude = [jnp.sqrt(a * a + b * b) for a, b in zip(real, imag)]
    part = held.shape[1]
    rows = min(part, width)
    for f in range(n_bins):
        near = [magnitude[g] for g in (f, f + 1, f - 1) if 0 <= g < n_bins]
        level = jnp.maximum(sum(near[1:], near[0]) / float(len(near)), 0.75)
        for p, values in ((0, real[f]), (1, imag[f])):
            white = (values / level).astype(jnp.bfloat16)
            for at in range(0, width, rows):
                piece, start = divmod(p * width + at, part)
                held[f * n_split + piece, start : start + rows] = white[at : at + rows]
    for chunk, out in zip(steps, row_outs):
        for i, step in enumerate(chunk):
            for s in range(n_split):
                out[0, i, s] = held[((q // n_split) ^ step) * n_split + s]
    for d, out in enumerate(piece_outs):
        out[...] = held[q ^ d]


def whiten(raw, n, n_split, steps):
    _, n_bins, width, channels = raw.shape
    part = 2 * width // n_split
    shapes = [(1, len(chunk), n_split, part, channels) for chunk in steps] + [(part, channels)] * n
    outs = pl.pallas_call(
        functools.partial(whiten_kernel, n, n_split, steps),
        out_shape=[jax.ShapeDtypeStruct(shape, jnp.bfloat16) for shape in shapes],
        in_specs=[pl.BlockSpec(memory_space=pltpu.VMEM)],
        out_specs=[pl.BlockSpec(memory_space=pltpu.VMEM)] * len(shapes),
        scratch_shapes=[pltpu.VMEM((n, part, channels), jnp.bfloat16)],
        compiler_params=pltpu.CompilerParams(vmem_limit_bytes=24 << 20),
        name="whiten",
    )(raw)
    return outs[: len(steps)], outs[len(steps) :]


def route_kernel(*refs):
    n = len(refs) // 2
    blocks, outs = refs[:n], refs[n:]
    q, z = lax.axis_index("row") // 2, lax.axis_index("col")
    for e, out in enumerate(outs):
        for d, block in enumerate(blocks):

            @pl.when((q ^ z ^ e) == d)
            def _(block=block, out=out):
                out[...] = block[...]


def route(blocks):
    n = len(blocks)
    shape = jax.ShapeDtypeStruct(blocks[0].shape, jnp.bfloat16)
    return pl.pallas_call(
        route_kernel,
        out_shape=[shape] * n,
        in_specs=[pl.BlockSpec(memory_space=pltpu.VMEM)] * n,
        out_specs=[pl.BlockSpec(memory_space=pltpu.VMEM)] * n,
        compiler_params=pltpu.CompilerParams(vmem_limit_bytes=24 << 20),
        name="route",
    )(*blocks)


def collect_kernel(*refs):
    for at, x in enumerate(refs[:-1]):
        refs[-1][at] = x[...]


def collect(parts):
    return pl.pallas_call(
        collect_kernel,
        out_shape=jax.ShapeDtypeStruct((len(parts), *parts[0].shape), jnp.bfloat16),
        in_specs=[pl.BlockSpec(memory_space=pltpu.VMEM)] * len(parts),
        out_specs=pl.BlockSpec(memory_space=pltpu.VMEM),
        cost_estimate=pl.CostEstimate(flops=1 << 33, bytes_accessed=0, transcendentals=0),
        compiler_params=pltpu.CompilerParams(vmem_limit_bytes=24 << 20),
        name="collect",
    )(*parts)


def turn_kernel(at, n, n_split, *refs):
    q = lax.axis_index("row") // 2
    out = refs[-1]
    where, bit = {0: (0, 0)}, n
    for ref in range(1, len(refs) - 1):
        bit //= 2
        for place, d in enumerate(list(where)):
            where[d ^ bit] = (ref, place)
    picked = []
    for s in range(n_split):
        for d in range(n):
            ref, place = where[d]
            own = s ^ (q % n_split)
            picked.append(refs[ref][place, at, own] if ref < 2 else refs[ref][place, own])
    out[...] = jnp.concatenate(picked, axis=0).T


def turn(at, parts, n):
    _, _, n_split, part, channels = parts[0].shape
    return pl.pallas_call(
        functools.partial(turn_kernel, at, n, n_split),
        out_shape=jax.ShapeDtypeStruct((channels, n * n_split * part), jnp.bfloat16),
        in_specs=[pl.BlockSpec(memory_space=pltpu.VMEM)] * len(parts),
        out_specs=pl.BlockSpec(memory_space=pltpu.VMEM),
        cost_estimate=pl.CostEstimate(flops=0, bytes_accessed=1, transcendentals=0),
        compiler_params=pltpu.CompilerParams(vmem_limit_bytes=24 << 20),
        name="turn",
    )(*parts)


def product_kernel(items, n, n_split, tile, norm, *refs):
    operands = [refs[at * (n_split + 1) : (at + 1) * (n_split + 1)] for at in range(len(items))]
    out, made, out_sem = refs[-3:]
    q, k = lax.axis_index("row") // 2, lax.axis_index("row") % 2
    channels = operands[0][0].shape[0]
    part = operands[0][1].shape[1]
    slots, _, height, width = made.shape
    per_column = channels // height
    n_tiles = per_column * (channels // width)
    pairs = [(s, d) for s in range(n_split) for d in range(n)]

    def store(item, at):
        step, other = items[item]
        block = 1 - k if other else k
        top = pl.multiple_of(at % per_column * height, height)
        start = pl.multiple_of(block * channels + at // per_column * width, width)
        slot = (item * n_tiles + at) % slots
        return pltpu.make_async_copy(
            made.at[slot],
            out.at[:, (q // n_split) ^ step, pl.ds(top, height), pl.ds(start, width)],
            out_sem.at[slot],
        )

    def one_tile(item, turned, columns, at):
        total = item * n_tiles + at

        @pl.when(total >= slots)
        def _():
            store(item, at).wait()

        left = turned[pl.ds(pl.multiple_of(at % per_column * height, height), height)]
        start = pl.multiple_of(at // per_column * width, width)
        piece = lambda s, d: columns[s][d, :, pl.ds(start, width)]
        right = jnp.concatenate([piece(s, d) for s, d in pairs], axis=0)
        made[total % slots, 0] = norm * jnp.dot(left, right, preferred_element_type=jnp.float32)
        half = part // 2 if n_split == 1 else n_split // 2
        crossed = []
        for s, d in pairs:
            if n_split == 1:
                values = piece(s, d)
                crossed += [-values[half:], values[:half]]
            else:
                sign = jnp.where((s ^ (q % n_split)) < half, -1.0, 1.0).astype(jnp.bfloat16)
                crossed.append(piece(s ^ half, d) * sign)
        right = jnp.concatenate(crossed, axis=0)
        made[total % slots, 1] = norm * jnp.dot(left, right, preferred_element_type=jnp.float32)
        store(item, at).start()

    for item, (turned, *columns) in enumerate(operands):
        lax.fori_loop(0, n_tiles, lambda at, _: one_tile(item, turned, columns, at), None)
    total = len(items) * n_tiles
    for at in range(max(0, total - slots), total):
        store(at // n_tiles, at % n_tiles).wait()


def product(items, turned, columns, before, n, n_split, n_bins):
    channels, depth = turned[0].shape
    width, height = min(256, channels), min(512, channels)
    slots = min(8, len(items) * (channels // width) * (channels // height))
    operands = [x for left, right in zip(turned, columns) for x in (left, *right)]
    specs = [pl.BlockSpec(memory_space=pltpu.VMEM)] * len(operands)
    aliases = {}
    if before is not None:
        aliases = {len(operands): 0}
        operands.append(before)
        specs.append(pl.BlockSpec(memory_space=pl.ANY))
    norm = 1.0 / math.sqrt(depth // 2)
    return pl.pallas_call(
        functools.partial(product_kernel, items, n, n_split, width, norm),
        out_shape=jax.ShapeDtypeStruct((2, n_bins, channels, 2 * channels), jnp.float32),
        in_specs=specs,
        out_specs=pl.BlockSpec(memory_space=pl.ANY),
        scratch_shapes=[
            pltpu.VMEM((slots, 2, height, width), jnp.float32),
            pltpu.SemaphoreType.DMA((slots,)),
        ],
        input_output_aliases=aliases,
        cost_estimate=pl.CostEstimate(
            flops=len(items) * 4 * channels * channels * depth // 4,
            bytes_accessed=len(items) * 8 * channels * channels // 4,
            transcendentals=0,
        ),
        compiler_params=pltpu.CompilerParams(vmem_limit_bytes=32 << 20),
        name="product",
    )(*operands)


def shards(spectra):
    n = lax.axis_size("col")
    n_bins = spectra.shape[1]
    assert lax.axis_size("row") == 2 * n and n % n_bins == 0 and n_bins > 1 and n & (n - 1) == 0
    n_split = n // n_bins
    chunks = [(0, 1)] + [tuple(range(2, n_bins))] * (n_bins > 2)
    place = [(at, i) for at, chunk in enumerate(chunks) for i in range(len(chunk))]
    rows, pieces = whiten(spectra, n, n_split, chunks)

    def along_line(values, bit):
        return lax.ppermute(values, "col", [(z, z ^ bit) for z in range(n)])

    def from_chip(values, d):
        return lax.ppermute(values, "row", [(2 * q + k, 2 * (q ^ d) + k) for q in range(n) for k in range(2)])

    def from_core(values):
        return lax.ppermute(values, "row", [(r, r ^ 1) for r in range(2 * n)])

    def gather_rows(own, first, at):
        parts, bit = [own[:, at], first[:, at]], n // 4
        while bit:
            parts.append(along_line(jnp.concatenate(parts), bit))
            bit //= 2
        return [own, first, *parts[2:]]

    def wait(values, done):
        return lax.optimization_barrier((values, done))

    def gather_bin(f):
        at, i = place[f]
        return gather_rows(rows[at], firsts[at], i)

    firsts = [along_line(rows[0], n // 2)]
    blocks = [from_chip(piece, d) if d else piece for d, piece in enumerate(pieces)]
    firsts, blocks = wait(firsts, blocks)
    arrived = [along_line(x, e) if e else x for e, x in enumerate(route(blocks))]
    firsts, arrived[1] = wait(firsts, arrived[1])
    parts = [gather_bin(0)]
    halves = [jnp.stack(arrived[: n // 2]), collect(arrived[n // 2 :])]
    direct = [d for d in range(1, n) if d & (d - 1) == 0]
    early = [from_chip(halves[0], d) for d in direct]
    (rows, firsts, early), halves = wait((rows, firsts, early), halves)
    near = [jnp.concatenate(halves)] + [None] * (n - 1)
    late = [from_chip(halves[1], d) for d in direct]
    for d in range(1, n_split):
        low = d & -d
        near[d] = jnp.concatenate([early[direct.index(d)], late[direct.index(d)]]) if d == low else from_chip(near[d ^ low], low)
    far = [from_core(x) for x in near[:n_split]]
    (rows, firsts), parts = wait((rows, firsts), parts)
    parts.append(gather_bin(1))
    firsts += [along_line(x, n // 2) for x in rows[1:2]]

    call = functools.partial(product, n=n, n_split=n_split, n_bins=n_bins)
    of_bin = lambda x, f: x[f * n_split : (f + 1) * n_split]
    turned = turn(0, parts[0], n)
    out = call([(0, False), (0, True)], [turned] * 2, [of_bin(near, 0), far], None)
    late, out = wait(late, out)
    for d in range(n_split, n):
        low = d & -d
        near[d] = jnp.concatenate([early[direct.index(d)], late[direct.index(d)]]) if d == low else from_chip(near[d ^ low], low)
    for f in range(1, n_bins):
        needed = (parts[f], firsts, rows, of_bin(near, f), of_bin(near, f + 1) if f + 2 < n_bins else [])
        (parts[f], firsts, rows, mine, later), out = wait(needed, out)
        turned = turn(place[f][1], parts[f], n)
        if f + 1 < n_bins:
            parts.append(gather_bin(f + 1))
        if f in (1, n_bins - 1):
            far = [from_core(x) for x in mine]
            following = [from_core(x) for x in later]
            out = call([(f, False)], [turned], [mine], out)
            (far, following), out = wait((far, following), out)
            out = call([(f, True)], [turned], [far], out)
        else:
            far, out = wait(following, out)
            following = [from_core(x) for x in later]
            out = call([(f, False), (f, True)], [turned] * 2, [mine, far], out)
    return out


def solution(mesh):
    in_specs = (P(None, None, "col", "row"),)
    out_specs = P(None, None, "row", "col")
    return jax.shard_map(shards, mesh=mesh, in_specs=in_specs, out_specs=out_specs, check_vma=False)
```

```python
import functools
import math

import jax
import jax.numpy as jnp
from jax import lax
from jax.experimental import pallas as pl
from jax.experimental.pallas import tpu as pltpu
from jax.sharding import PartitionSpec as P


def whiten_kernel(n, n_split, steps, raw, *refs):
    n_bins, width = raw.shape[1], raw.shape[2]
    row_outs, piece_outs, held = refs[: len(steps)], refs[len(steps) : -1], refs[-1]
    q = lax.axis_index("row") // 2
    real = [raw[0, f].astype(jnp.float32) for f in range(n_bins)]
    imag = [raw[1, f].astype(jnp.float32) for f in range(n_bins)]
    magnitude = [jnp.sqrt(a * a + b * b) for a, b in zip(real, imag)]
    part = held.shape[1]
    rows = min(part, width)
    for f in range(n_bins):
        near = [magnitude[g] for g in (f, f + 1, f - 1) if 0 <= g < n_bins]
        level = jnp.maximum(sum(near[1:], near[0]) / float(len(near)), 0.75)
        for p, values in ((0, real[f]), (1, imag[f])):
            white = (values / level).astype(jnp.bfloat16)
            for at in range(0, width, rows):
                piece, start = divmod(p * width + at, part)
                held[f * n_split + piece, start : start + rows] = white[at : at + rows]
    for chunk, out in zip(steps, row_outs):
        for i, step in enumerate(chunk):
            for s in range(n_split):
                out[0, i, s] = held[((q // n_split) ^ step) * n_split + s]
    for d, out in enumerate(piece_outs):
        out[...] = held[q ^ d]


def whiten(raw, n, n_split, steps):
    _, n_bins, width, channels = raw.shape
    part = 2 * width // n_split
    shapes = [(1, len(chunk), n_split, part, channels) for chunk in steps] + [(part, channels)] * n
    outs = pl.pallas_call(
        functools.partial(whiten_kernel, n, n_split, steps),
        out_shape=[jax.ShapeDtypeStruct(shape, jnp.bfloat16) for shape in shapes],
        in_specs=[pl.BlockSpec(memory_space=pltpu.VMEM)],
        out_specs=[pl.BlockSpec(memory_space=pltpu.VMEM)] * len(shapes),
        scratch_shapes=[pltpu.VMEM((n, part, channels), jnp.bfloat16)],
        compiler_params=pltpu.CompilerParams(vmem_limit_bytes=24 << 20),
        name="whiten",
    )(raw)
    return outs[: len(steps)], outs[len(steps) :]


def route_kernel(*refs):
    n = len(refs) // 2
    blocks, outs = refs[:n], refs[n:]
    q, z = lax.axis_index("row") // 2, lax.axis_index("col")
    for e, out in enumerate(outs):
        for d, block in enumerate(blocks):

            @pl.when((q ^ z ^ e) == d)
            def _(block=block, out=out):
                out[...] = block[...]


def route(blocks):
    n = len(blocks)
    shape = jax.ShapeDtypeStruct(blocks[0].shape, jnp.bfloat16)
    return pl.pallas_call(
        route_kernel,
        out_shape=[shape] * n,
        in_specs=[pl.BlockSpec(memory_space=pltpu.VMEM)] * n,
        out_specs=[pl.BlockSpec(memory_space=pltpu.VMEM)] * n,
        compiler_params=pltpu.CompilerParams(vmem_limit_bytes=24 << 20),
        name="route",
    )(*blocks)


def collect_kernel(*refs):
    for at, x in enumerate(refs[:-1]):
        refs[-1][at] = x[...]


def collect(parts):
    return pl.pallas_call(
        collect_kernel,
        out_shape=jax.ShapeDtypeStruct((len(parts), *parts[0].shape), jnp.bfloat16),
        in_specs=[pl.BlockSpec(memory_space=pltpu.VMEM)] * len(parts),
        out_specs=pl.BlockSpec(memory_space=pltpu.VMEM),
        cost_estimate=pl.CostEstimate(flops=1 << 33, bytes_accessed=0, transcendentals=0),
        compiler_params=pltpu.CompilerParams(vmem_limit_bytes=24 << 20),
        name="collect",
    )(*parts)


def turn_kernel(at, n, n_split, *refs):
    q = lax.axis_index("row") // 2
    out = refs[-1]
    where, bit = {0: (0, 0)}, n
    for ref in range(1, len(refs) - 1):
        bit //= 2
        for place, d in enumerate(list(where)):
            where[d ^ bit] = (ref, place)
    picked = []
    for s in range(n_split):
        for d in range(n):
            ref, place = where[d]
            own = s ^ (q % n_split)
            picked.append(refs[ref][place, at, own] if len(refs[ref].shape) == 5 else refs[ref][place, own])
    out[...] = jnp.concatenate(picked, axis=0).T


def turn(at, parts, n):
    _, _, n_split, part, channels = parts[0].shape
    return pl.pallas_call(
        functools.partial(turn_kernel, at, n, n_split),
        out_shape=jax.ShapeDtypeStruct((channels, n * n_split * part), jnp.bfloat16),
        in_specs=[pl.BlockSpec(memory_space=pltpu.VMEM)] * len(parts),
        out_specs=pl.BlockSpec(memory_space=pltpu.VMEM),
        cost_estimate=pl.CostEstimate(flops=0, bytes_accessed=1, transcendentals=0),
        compiler_params=pltpu.CompilerParams(vmem_limit_bytes=24 << 20),
        name="turn",
    )(*parts)


def product_kernel(items, n, n_split, tile, norm, *refs):
    operands = [refs[at * (n_split + 1) : (at + 1) * (n_split + 1)] for at in range(len(items))]
    out, made, out_sem = refs[-3:]
    q, k = lax.axis_index("row") // 2, lax.axis_index("row") % 2
    channels = operands[0][0].shape[0]
    part = operands[0][1].shape[1]
    slots, _, height, width = made.shape
    per_column = channels // height
    n_tiles = per_column * (channels // width)
    pairs = [(s, d) for s in range(n_split) for d in range(n)]

    def store(item, at):
        step, other = items[item]
        block = 1 - k if other else k
        top = pl.multiple_of(at % per_column * height, height)
        start = pl.multiple_of(block * channels + at // per_column * width, width)
        slot = (item * n_tiles + at) % slots
        return pltpu.make_async_copy(
            made.at[slot],
            out.at[:, (q // n_split) ^ step, pl.ds(top, height), pl.ds(start, width)],
            out_sem.at[slot],
        )

    def one_tile(item, turned, columns, at):
        total = item * n_tiles + at

        @pl.when(total >= slots)
        def _():
            store(item, at).wait()

        left = turned[pl.ds(pl.multiple_of(at % per_column * height, height), height)]
        start = pl.multiple_of(at // per_column * width, width)
        piece = lambda s, d: columns[s][d, :, pl.ds(start, width)]
        right = jnp.concatenate([piece(s, d) for s, d in pairs], axis=0)
        made[total % slots, 0] = norm * jnp.dot(left, right, preferred_element_type=jnp.float32)
        half = part // 2 if n_split == 1 else n_split // 2
        crossed = []
        for s, d in pairs:
            if n_split == 1:
                values = piece(s, d)
                crossed += [-values[half:], values[:half]]
            else:
                sign = jnp.where((s ^ (q % n_split)) < half, -1.0, 1.0).astype(jnp.bfloat16)
                crossed.append(piece(s ^ half, d) * sign)
        right = jnp.concatenate(crossed, axis=0)
        made[total % slots, 1] = norm * jnp.dot(left, right, preferred_element_type=jnp.float32)
        store(item, at).start()

    for item, (turned, *columns) in enumerate(operands):
        lax.fori_loop(0, n_tiles, lambda at, _: one_tile(item, turned, columns, at), None)
    total = len(items) * n_tiles
    for at in range(max(0, total - slots), total):
        store(at // n_tiles, at % n_tiles).wait()


def product(items, turned, columns, before, n, n_split, n_bins):
    channels, depth = turned[0].shape
    width, height = min(256, channels), min(512, channels)
    slots = min(8, len(items) * (channels // width) * (channels // height))
    operands = [x for left, right in zip(turned, columns) for x in (left, *right)]
    specs = [pl.BlockSpec(memory_space=pltpu.VMEM)] * len(operands)
    aliases = {}
    if before is not None:
        aliases = {len(operands): 0}
        operands.append(before)
        specs.append(pl.BlockSpec(memory_space=pl.ANY))
    norm = 1.0 / math.sqrt(depth // 2)
    return pl.pallas_call(
        functools.partial(product_kernel, items, n, n_split, width, norm),
        out_shape=jax.ShapeDtypeStruct((2, n_bins, channels, 2 * channels), jnp.float32),
        in_specs=specs,
        out_specs=pl.BlockSpec(memory_space=pl.ANY),
        scratch_shapes=[
            pltpu.VMEM((slots, 2, height, width), jnp.float32),
            pltpu.SemaphoreType.DMA((slots,)),
        ],
        input_output_aliases=aliases,
        cost_estimate=pl.CostEstimate(
            flops=len(items) * 4 * channels * channels * depth // 4,
            bytes_accessed=len(items) * 8 * channels * channels // 4,
            transcendentals=0,
        ),
        compiler_params=pltpu.CompilerParams(vmem_limit_bytes=32 << 20),
        name="product",
    )(*operands)


def shards(spectra):
    n = lax.axis_size("col")
    n_bins = spectra.shape[1]
    assert lax.axis_size("row") == 2 * n and n % n_bins == 0 and n_bins > 1 and n & (n - 1) == 0
    n_split = n // n_bins
    chunks = [(0, 1)] + [tuple(range(2, n_bins))] * (n_bins > 2)
    place = [(at, i) for at, chunk in enumerate(chunks) for i in range(len(chunk))]
    rows, pieces = whiten(spectra, n, n_split, chunks)

    def along_line(values, bit):
        return lax.ppermute(values, "col", [(z, z ^ bit) for z in range(n)])

    def from_chip(values, d):
        return lax.ppermute(values, "row", [(2 * q + k, 2 * (q ^ d) + k) for q in range(n) for k in range(2)])

    def from_core(values):
        return lax.ppermute(values, "row", [(r, r ^ 1) for r in range(2 * n)])

    def gather_rows(parts):
        parts, bit = list(parts), n // 4
        while bit:
            parts.append(along_line(jnp.concatenate(parts), bit))
            bit //= 2
        return parts

    def wait(values, done):
        return lax.optimization_barrier((values, done))

    def gather_bin(f):
        at, i = place[f]
        return [rows[at], firsts[at], *gather_rows([rows[at][:, i], firsts[at][:, i]])[2:]]

    firsts = [along_line(rows[0], n // 2)]
    blocks = [from_chip(piece, d) if d else piece for d, piece in enumerate(pieces)]
    firsts, blocks = wait(firsts, blocks)
    arrived = [along_line(x, e) if e else x for e, x in enumerate(route(blocks))]
    firsts, arrived[1] = wait(firsts, arrived[1])
    parts = [gather_rows([rows[0], firsts[0]])]
    halves = [jnp.stack(arrived[: n // 2]), collect(arrived[n // 2 :])]
    direct = [d for d in range(1, n) if d & (d - 1) == 0]
    early = [from_chip(halves[0], d) for d in direct]
    (rows, firsts, early), halves = wait((rows, firsts, early), halves)
    near = [jnp.concatenate(halves)] + [None] * (n - 1)
    late = [from_chip(halves[1], d) for d in direct]
    for d in range(1, n_split):
        low = d & -d
        near[d] = jnp.concatenate([early[direct.index(d)], late[direct.index(d)]]) if d == low else from_chip(near[d ^ low], low)
    far = [from_core(x) for x in near[:n_split]]
    parts.append(parts[0])
    firsts += [along_line(x, n // 2) for x in rows[1:2]]

    call = functools.partial(product, n=n, n_split=n_split, n_bins=n_bins)
    of_bin = lambda x, f: x[f * n_split : (f + 1) * n_split]
    turned = turn(0, parts[0], n)
    out = call([(0, False), (0, True)], [turned] * 2, [of_bin(near, 0), far], None)
    late, out = wait(late, out)
    for d in range(n_split, n):
        low = d & -d
        near[d] = jnp.concatenate([early[direct.index(d)], late[direct.index(d)]]) if d == low else from_chip(near[d ^ low], low)
    for f in range(1, n_bins):
        needed = (parts[f], firsts, rows, of_bin(near, f), of_bin(near, f + 1) if f + 2 < n_bins else [])
        (parts[f], firsts, rows, mine, later), out = wait(needed, out)
        turned = turn(place[f][1], parts[f], n)
        if f + 1 < n_bins:
            parts.append(gather_bin(f + 1))
        if f in (1, n_bins - 1):
            far = [from_core(x) for x in mine]
            following = [from_core(x) for x in later]
            out = call([(f, False)], [turned], [mine], out)
            (far, following), out = wait((far, following), out)
            out = call([(f, True)], [turned], [far], out)
        else:
            far, out = wait(following, out)
            following = [from_core(x) for x in later]
            out = call([(f, False), (f, True)], [turned] * 2, [mine, far], out)
    return out


def solution(mesh):
    in_specs = (P(None, None, "col", "row"),)
    out_specs = P(None, None, "row", "col")
    return jax.shard_map(shards, mesh=mesh, in_specs=in_specs, out_specs=out_specs, check_vma=False)
```

```python
import functools
import math

import jax
import jax.numpy as jnp
from jax import lax
from jax.experimental import pallas as pl
from jax.experimental.pallas import tpu as pltpu
from jax.sharding import PartitionSpec as P


def whiten_kernel(n, n_split, steps, raw, *refs):
    n_bins, width = raw.shape[1], raw.shape[2]
    row_outs, piece_outs, held = refs[: len(steps)], refs[len(steps) : -1], refs[-1]
    q = lax.axis_index("row") // 2
    real = [raw[0, f].astype(jnp.float32) for f in range(n_bins)]
    imag = [raw[1, f].astype(jnp.float32) for f in range(n_bins)]
    magnitude = [jnp.sqrt(a * a + b * b) for a, b in zip(real, imag)]
    part = held.shape[1]
    rows = min(part, width)
    for f in range(n_bins):
        near = [magnitude[g] for g in (f, f + 1, f - 1) if 0 <= g < n_bins]
        level = jnp.maximum(sum(near[1:], near[0]) / float(len(near)), 0.75)
        for p, values in ((0, real[f]), (1, imag[f])):
            white = (values / level).astype(jnp.bfloat16)
            for at in range(0, width, rows):
                piece, start = divmod(p * width + at, part)
                held[f * n_split + piece, start : start + rows] = white[at : at + rows]
    for chunk, out in zip(steps, row_outs):
        for i, step in enumerate(chunk):
            for s in range(n_split):
                out[0, i, s] = held[((q // n_split) ^ step) * n_split + s]
    for d, out in enumerate(piece_outs):
        out[...] = held[q ^ d]


def whiten(raw, n, n_split, steps):
    _, n_bins, width, channels = raw.shape
    part = 2 * width // n_split
    shapes = [(1, len(chunk), n_split, part, channels) for chunk in steps] + [(part, channels)] * n
    outs = pl.pallas_call(
        functools.partial(whiten_kernel, n, n_split, steps),
        out_shape=[jax.ShapeDtypeStruct(shape, jnp.bfloat16) for shape in shapes],
        in_specs=[pl.BlockSpec(memory_space=pltpu.VMEM)],
        out_specs=[pl.BlockSpec(memory_space=pltpu.VMEM)] * len(shapes),
        scratch_shapes=[pltpu.VMEM((n, part, channels), jnp.bfloat16)],
        compiler_params=pltpu.CompilerParams(vmem_limit_bytes=24 << 20),
        name="whiten",
    )(raw)
    return outs[: len(steps)], outs[len(steps) :]


def route_kernel(*refs):
    n = len(refs) // 2
    blocks, outs = refs[:n], refs[n:]
    q, z = lax.axis_index("row") // 2, lax.axis_index("col")
    for e, out in enumerate(outs):
        for d, block in enumerate(blocks):

            @pl.when((q ^ z ^ e) == d)
            def _(block=block, out=out):
                out[...] = block[...]


def route(blocks):
    n = len(blocks)
    shape = jax.ShapeDtypeStruct(blocks[0].shape, jnp.bfloat16)
    return pl.pallas_call(
        route_kernel,
        out_shape=[shape] * n,
        in_specs=[pl.BlockSpec(memory_space=pltpu.VMEM)] * n,
        out_specs=[pl.BlockSpec(memory_space=pltpu.VMEM)] * n,
        compiler_params=pltpu.CompilerParams(vmem_limit_bytes=24 << 20),
        name="route",
    )(*blocks)


def collect_kernel(*refs):
    for at, x in enumerate(refs[:-1]):
        refs[-1][at] = x[...]


def collect(parts):
    return pl.pallas_call(
        collect_kernel,
        out_shape=jax.ShapeDtypeStruct((len(parts), *parts[0].shape), jnp.bfloat16),
        in_specs=[pl.BlockSpec(memory_space=pltpu.VMEM)] * len(parts),
        out_specs=pl.BlockSpec(memory_space=pltpu.VMEM),
        cost_estimate=pl.CostEstimate(flops=1 << 33, bytes_accessed=0, transcendentals=0),
        compiler_params=pltpu.CompilerParams(vmem_limit_bytes=24 << 20),
        name="collect",
    )(*parts)


def turn_kernel(at, n, n_split, *refs):
    q = lax.axis_index("row") // 2
    out = refs[-1]
    where, bit = {0: (0, 0)}, n
    for ref in range(1, len(refs) - 1):
        bit //= 2
        for place, d in enumerate(list(where)):
            where[d ^ bit] = (ref, place)
    picked = []
    for s in range(n_split):
        for d in range(n):
            ref, place = where[d]
            own = s ^ (q % n_split)
            picked.append(refs[ref][place, at, own] if len(refs[ref].shape) == 5 else refs[ref][place, own])
    out[...] = jnp.concatenate(picked, axis=0).T


def turn(at, parts, n):
    _, _, n_split, part, channels = parts[0].shape
    return pl.pallas_call(
        functools.partial(turn_kernel, at, n, n_split),
        out_shape=jax.ShapeDtypeStruct((channels, n * n_split * part), jnp.bfloat16),
        in_specs=[pl.BlockSpec(memory_space=pltpu.VMEM)] * len(parts),
        out_specs=pl.BlockSpec(memory_space=pltpu.VMEM),
        cost_estimate=pl.CostEstimate(flops=0, bytes_accessed=1, transcendentals=0),
        compiler_params=pltpu.CompilerParams(vmem_limit_bytes=24 << 20),
        name="turn",
    )(*parts)


def product_kernel(items, n, n_split, tile, norm, *refs):
    operands = [refs[at * (n_split + 1) : (at + 1) * (n_split + 1)] for at in range(len(items))]
    out, made, out_sem = refs[-3:]
    q, k = lax.axis_index("row") // 2, lax.axis_index("row") % 2
    channels = operands[0][0].shape[0]
    part = operands[0][1].shape[1]
    slots, _, height, width = made.shape
    per_column = channels // height
    n_tiles = per_column * (channels // width)
    pairs = [(s, d) for s in range(n_split) for d in range(n)]

    def store(item, at):
        step, other = items[item]
        block = 1 - k if other else k
        top = pl.multiple_of(at % per_column * height, height)
        start = pl.multiple_of(block * channels + at // per_column * width, width)
        slot = (item * n_tiles + at) % slots
        return pltpu.make_async_copy(
            made.at[slot],
            out.at[:, (q // n_split) ^ step, pl.ds(top, height), pl.ds(start, width)],
            out_sem.at[slot],
        )

    def one_tile(item, turned, columns, at):
        total = item * n_tiles + at

        @pl.when(total >= slots)
        def _():
            store(item, at).wait()

        left = turned[pl.ds(pl.multiple_of(at % per_column * height, height), height)]
        start = pl.multiple_of(at // per_column * width, width)
        piece = lambda s, d: columns[s][d, :, pl.ds(start, width)]
        right = jnp.concatenate([piece(s, d) for s, d in pairs], axis=0)
        made[total % slots, 0] = norm * jnp.dot(left, right, preferred_element_type=jnp.float32)
        half = part // 2 if n_split == 1 else n_split // 2
        crossed = []
        for s, d in pairs:
            if n_split == 1:
                values = piece(s, d)
                crossed += [-values[half:], values[:half]]
            else:
                sign = jnp.where((s ^ (q % n_split)) < half, -1.0, 1.0).astype(jnp.bfloat16)
                crossed.append(piece(s ^ half, d) * sign)
        right = jnp.concatenate(crossed, axis=0)
        made[total % slots, 1] = norm * jnp.dot(left, right, preferred_element_type=jnp.float32)
        store(item, at).start()

    for item, (turned, *columns) in enumerate(operands):
        lax.fori_loop(0, n_tiles, lambda at, _: one_tile(item, turned, columns, at), None)
    total = len(items) * n_tiles
    for at in range(max(0, total - slots), total):
        store(at // n_tiles, at % n_tiles).wait()


def product(items, turned, columns, before, n, n_split, n_bins):
    channels, depth = turned[0].shape
    width, height = min(256, channels), min(512, channels)
    slots = min(8, len(items) * (channels // width) * (channels // height))
    operands = [x for left, right in zip(turned, columns) for x in (left, *right)]
    specs = [pl.BlockSpec(memory_space=pltpu.VMEM)] * len(operands)
    aliases = {}
    if before is not None:
        aliases = {len(operands): 0}
        operands.append(before)
        specs.append(pl.BlockSpec(memory_space=pl.ANY))
    norm = 1.0 / math.sqrt(depth // 2)
    return pl.pallas_call(
        functools.partial(product_kernel, items, n, n_split, width, norm),
        out_shape=jax.ShapeDtypeStruct((2, n_bins, channels, 2 * channels), jnp.float32),
        in_specs=specs,
        out_specs=pl.BlockSpec(memory_space=pl.ANY),
        scratch_shapes=[
            pltpu.VMEM((slots, 2, height, width), jnp.float32),
            pltpu.SemaphoreType.DMA((slots,)),
        ],
        input_output_aliases=aliases,
        cost_estimate=pl.CostEstimate(
            flops=len(items) * 4 * channels * channels * depth // 4,
            bytes_accessed=len(items) * 8 * channels * channels // 4,
            transcendentals=0,
        ),
        compiler_params=pltpu.CompilerParams(vmem_limit_bytes=32 << 20),
        name="product",
    )(*operands)


def shards(spectra):
    n = lax.axis_size("col")
    n_bins = spectra.shape[1]
    assert lax.axis_size("row") == 2 * n and n % n_bins == 0 and n_bins > 1 and n & (n - 1) == 0
    n_split = n // n_bins
    chunks = [(0, 1)] + [tuple(range(2, n_bins))] * (n_bins > 2)
    place = [(at, i) for at, chunk in enumerate(chunks) for i in range(len(chunk))]
    rows, pieces = whiten(spectra, n, n_split, chunks)

    def along_line(values, bit):
        return lax.ppermute(values, "col", [(z, z ^ bit) for z in range(n)])

    def from_chip(values, d):
        return lax.ppermute(values, "row", [(2 * q + k, 2 * (q ^ d) + k) for q in range(n) for k in range(2)])

    def from_core(values):
        return lax.ppermute(values, "row", [(r, r ^ 1) for r in range(2 * n)])

    def gather_rows(parts):
        parts, bit = list(parts), n // 4
        while bit:
            parts.append(along_line(jnp.concatenate(parts), bit))
            bit //= 2
        return parts

    def wait(values, done):
        return lax.optimization_barrier((values, done))

    def gather_bin(f):
        at, i = place[f]
        return [rows[at], firsts[at], *gather_rows([rows[at][:, i], firsts[at][:, i]])[2:]]

    firsts = [along_line(rows[0], n // 2)]
    blocks = [from_chip(piece, d) if d else piece for d, piece in enumerate(pieces)]
    firsts, blocks = wait(firsts, blocks)
    arrived = [along_line(x, e) if e else x for e, x in enumerate(route(blocks))]
    firsts, arrived[1] = wait(firsts, arrived[1])
    parts = [gather_rows([rows[0], firsts[0]])]
    held = collect(arrived)
    (rows, firsts), held = wait((rows, firsts), held)
    near = [held] + [None] * (n - 1)
    direct = [d for d in range(1, n) if d & (d - 1) == 0]
    for d in range(1, n):
        if d in direct or d < n_split:
            near[d] = from_chip(near[d ^ (d & -d)], d & -d)
    far = [from_core(x) for x in near[:n_split]]
    parts.append(parts[0])
    firsts += [along_line(x, n // 2) for x in rows[1:2]]

    call = functools.partial(product, n=n, n_split=n_split, n_bins=n_bins)
    of_bin = lambda x, f: x[f * n_split : (f + 1) * n_split]
    turned = turn(0, parts[0], n)
    out = call([(0, False), (0, True)], [turned] * 2, [of_bin(near, 0), far], None)
    near[n_split:], out = wait(near[n_split:], out)
    for d in range(n_split, n):
        if near[d] is None:
            near[d] = from_chip(near[d ^ (d & -d)], d & -d)
    for f in range(1, n_bins):
        needed = (parts[f], firsts, rows, of_bin(near, f), of_bin(near, f + 1) if f + 2 < n_bins else [])
        (parts[f], firsts, rows, mine, later), out = wait(needed, out)
        turned = turn(place[f][1], parts[f], n)
        if f + 1 < n_bins:
            parts.append(gather_bin(f + 1))
        if f in (1, n_bins - 1):
            far = [from_core(x) for x in mine]
            following = [from_core(x) for x in later]
            out = call([(f, False)], [turned], [mine], out)
            (far, following), out = wait((far, following), out)
            out = call([(f, True)], [turned], [far], out)
        else:
            far, out = wait(following, out)
            following = [from_core(x) for x in later]
            out = call([(f, False), (f, True)], [turned] * 2, [mine, far], out)
    return out


def solution(mesh):
    in_specs = (P(None, None, "col", "row"),)
    out_specs = P(None, None, "row", "col")
    return jax.shard_map(shards, mesh=mesh, in_specs=in_specs, out_specs=out_specs, check_vma=False)
```
